512 devices in a mesh: grp: 8 (over z_hi, core), pair: 64 (over y, x, z_lo).
Axes of the slice: x: 4, y: 4, z: 16 (z_hi: 4, z_lo: 4; z = z_hi * 4 + z_lo), core: 2. Of those that a mesh axis runs over, the one named last changes fastest.
Arguments:
- embeddings: bfloat16 [786432, 768], P(('grp', 'pair')), parts along dimension 0
- cluster_ids: int32 [786432], P(('grp', 'pair')), parts along dimension 0, may hold values from 0 to 3, as said below
- row_counts: int32 [512], P(('grp', 'pair')), parts along dimension 0, may hold values from 1 to 1536, 73728 in all
Outputs:
- best_cosine: float32 [786432], P(('grp', 'pair')), parts along dimension 0
The draws below stay inside these ranges and needn't reach their ends.
There are 8 independent parts, one for each index of `grp`. The reference program is written for one: setup_inputs(seed, part) draws one part's arguments, and reference() takes and returns one part's arrays. A program takes and returns all parts, laid end to end along the dimension named above; each array names one. Nothing has to cross between parts.
Inputs may be any that keep to these rules, and one draw needn't show every extreme that they name: `cluster_ids`: every cluster number occurs.
All inputs are finite; a program needn't handle non-finite values. No bound on the sum of `row_counts` on one device may be relied on, other than what follows from the above.
Results may differ from the reference program's by a relative error of at most 0.00037.
Values may be sent and summed in bfloat16 or wider, within the bound.
No kernel may reach another device: no remote copies, remote signals or barrier semaphores. Data moves between devices by JAX's collectives and lax.ppermute only.
A program may use at most 64 MiB of HBM per device.

```python
import math
import jax
import jax.numpy as jnp
import numpy as np
from jax import lax

D = 768
ROWS = 1536
CLUSTERS = 4
ROUNDS = 4
ROWS_ALL = 98304
N_PAIR = 64


def cluster_helper(key):
    key_major, key_minor = jax.random.split(key)
    major = jax.random.randint(key_major, (ROWS_ALL,), 0, 4, dtype=jnp.int32)
    minor = jax.random.randint(key_minor, (ROWS_ALL,), 1, CLUSTERS, dtype=jnp.int32)
    member = jnp.where(major > 0, 0, minor).astype(jnp.int32)
    return member.at[:CLUSTERS].set(jnp.arange(CLUSTERS, dtype=jnp.int32))


def draw_cluster_ids(key, part):
    return cluster_helper(key)


def draw_embeddings(key, part):
    member = cluster_helper(key)
    key = jax.random.fold_in(key, 7)
    key_center, key_strength, key_noise = jax.random.split(key, 3)
    centers = jax.random.normal(key_center, (CLUSTERS, D), jnp.float32)
    strength = jnp.exp(jax.random.uniform(key_strength, (CLUSTERS,), jnp.float32, jnp.log(0.2), jnp.log(3.0)))
    noise = jax.random.normal(key_noise, (ROWS_ALL, D), jnp.float32)
    rows = centers[member] * strength[member][:, None] + noise
    return rows.astype(jnp.bfloat16)


def profile(count, total, bound, skew):
    loads = [(1 << 20) // math.isqrt(standing ** skew) + 1 for standing in range(2, count + 1)]
    spare, given = total - bound - (count - 1), [1] * (count - 1)
    while spare > 0:
        free = [i for i in range(count - 1) if given[i] < bound]
        whole, budget = sum([loads[i] for i in free]), spare
        for i in free:
            more = min(bound - given[i], max(1, budget * loads[i] // whole), spare)
            given[i] = given[i] + more
            spare = spare - more
    return np.array([bound] + given)


def ragged_sizes(stream_key, number_of, total, reach, skew):
    if number_of == 2:
        one = jax.random.randint(stream_key, (), max(1, total - reach), min(reach, total - 1) + 1)
        return jnp.stack([one, total - one])
    lengths = jnp.asarray(profile(number_of, total, reach, skew), jnp.int32)
    pairs = (number_of - 1) // 2
    donor, sink = lengths[1:1 + 2 * pairs:2], lengths[2:2 + 2 * pairs:2]
    slack = jnp.minimum(donor - 1, reach - sink)
    passed = jax.random.randint(jax.random.fold_in(stream_key, 1), (pairs,), 0, 1 << 20) % (slack + 1)
    lengths = lengths.at[1:1 + 2 * pairs:2].set(donor - passed).at[2:2 + 2 * pairs:2].set(sink + passed)
    return lengths[jax.random.permutation(jax.random.fold_in(stream_key, 2), number_of)]


def setup_inputs(seed: int = 0, part: int = 0) -> dict:
    key_of = jax.random.split(jax.random.key(seed), 4)
    part_splits = jax.random.split(jax.random.fold_in(key_of[3], part), 4)
    return {
        "embeddings": draw_embeddings(jax.random.fold_in(jax.random.fold_in(key_of[3], part), 71), part),
        "cluster_ids": draw_cluster_ids(jax.random.fold_in(jax.random.fold_in(key_of[3], part), 71), part),
        "row_counts": ragged_sizes(part_splits[2], N_PAIR, N_PAIR * ROWS * 3 // 4, ROWS, 2).astype(jnp.int32),
    }


def reference(embeddings, cluster_ids, row_counts):
    wide = embeddings.astype(jnp.float32)
    squared = lax.optimization_barrier(jnp.sum(wide * wide, axis=1, keepdims=True))
    normed = (wide * lax.rsqrt(squared + 1e-06)).astype(jnp.bfloat16)
    position = jnp.arange(ROWS_ALL, dtype=jnp.int32)
    owner = position // ROWS
    valid = position % ROWS < row_counts[owner]
    tag = jnp.where(valid, cluster_ids, -1).astype(jnp.int32)

    def one_block(block):
        start = (block * ROWS).astype(jnp.int32)
        own = lax.dynamic_slice_in_dim(normed, start, ROWS, 0)
        own_tag = lax.dynamic_slice_in_dim(tag, start, ROWS, 0)
        best = jnp.full((ROWS,), -1.0, jnp.float32)
        for step in range(ROUNDS):
            other = jnp.bitwise_xor(block, N_PAIR >> step + 1).astype(jnp.int32)
            other_start = (other * ROWS).astype(jnp.int32)
            part = lax.dynamic_slice_in_dim(normed, other_start, ROWS, 0)
            part_tag = lax.dynamic_slice_in_dim(tag, other_start, ROWS, 0)
            tile = jnp.dot(own, part.T, preferred_element_type=jnp.float32)
            same = (own_tag[:, None] == part_tag[None, :]) & (own_tag[:, None] >= 0)
            tile = jnp.where(same, tile, -1.0)
            best = jnp.maximum(best, lax.optimization_barrier(jnp.max(tile, axis=1)))
        return best
    result = lax.map(one_block, jnp.arange(N_PAIR, dtype=jnp.int32))
    return result.reshape(ROWS_ALL)
```

```python
import functools

import jax
import jax.numpy as jnp
from jax import lax
from jax.experimental import pallas as pl
from jax.experimental.pallas import tpu as pltpu
from jax.sharding import PartitionSpec as P

LANES = 128
TAG_ROWS = 16
CHUNKS = (512, 768, 256)
AXES = ("grp", "pair")


def routes(grp, pair):
    side = 4
    rest = pair // (side * side)
    near, far = [], []
    for g in range(grp):
        for y in range(side):
            for x in range(side):
                for z in range(rest):

                    def at(v, u):
                        return g * pair + (v * side + u) * rest + z

                    owns_y = (y in (1, 2)) ^ (x in (1, 2)) ^ (g % 2 == 1)
                    here = at(y, x)
                    near.append((here, at(y, x ^ 1) if owns_y else at(y ^ 1, x)))
                    far.append((here, at(3 - y, x) if owns_y else at(y, 3 - x)))
    return near, far


def normalize(tagged, first, count):
    def kernel(*refs):
        if tagged:
            count_ref, ids_ref, rows_ref, out_ref = refs
        else:
            rows_ref, out_ref = refs
        wide = rows_ref[...].astype(jnp.float32)
        squared = jnp.sum(wide * wide, axis=1, keepdims=True)
        out_ref[0:count, :] = (wide * lax.rsqrt(squared + 1e-06)).astype(jnp.bfloat16)
        if tagged:
            ids = ids_ref[...]
            place = lax.broadcasted_iota(jnp.int32, ids.shape, 0) * LANES
            place = place + lax.broadcasted_iota(jnp.int32, ids.shape, 1)
            tags = jnp.where(place < count_ref[0], ids, -1).astype(jnp.float32)
            spare = jnp.full((TAG_ROWS - ids.shape[0], LANES), -1.0, jnp.float32)
            tags = jnp.concatenate([tags, spare], axis=0).astype(jnp.bfloat16)
            out_ref[count:, 0:LANES] = tags
            out_ref[count:, LANES:] = jnp.zeros((TAG_ROWS, out_ref.shape[1] - LANES), jnp.bfloat16)

    def call(rows, *extra):
        width = rows.shape[1]
        step = count if tagged else 256
        total = count + (TAG_ROWS if tagged else 0)
        specs = [pl.BlockSpec((step, width), lambda i: (i + first // step, 0))]
        if tagged:
            specs = [
                pl.BlockSpec(memory_space=pltpu.SMEM),
                pl.BlockSpec(extra[1].shape, lambda i: (0, 0)),
            ] + specs
        return pl.pallas_call(
            kernel if tagged else kernel_of_step(step),
            grid=(count // step,),
            in_specs=specs,
            out_specs=pl.BlockSpec((total if tagged else step, width), lambda i: (i, 0)),
            out_shape=jax.ShapeDtypeStruct((total, width), jnp.bfloat16),
            cost_estimate=pl.CostEstimate(flops=4 * count * width, bytes_accessed=4 * count * width, transcendentals=count),
            name="normalize",
        )(*extra, rows)

    def kernel_of_step(step):
        def body(rows_ref, out_ref):
            wide = rows_ref[...].astype(jnp.float32)
            squared = jnp.sum(wide * wide, axis=1, keepdims=True)
            out_ref[...] = (wide * lax.rsqrt(squared + 1e-06)).astype(jnp.bfloat16)

        return body

    return call


def products_kernel(plan, n_own, n_far, n_near, *refs):
    refs = list(refs)
    own_tag, far_tag, near_tag = refs[:3]
    state_in = refs[3:6]
    chunks = refs[6 : 6 + n_own + n_far + n_near]
    state_out = refs[6 + n_own + n_far + n_near : 9 + n_own + n_far + n_near]
    racc, cacc = refs[-2:]
    rows, cols, pairs, block = plan
    near_tags = near_tag[...].astype(jnp.float32)
    near_tags = jnp.where(near_tags < 0.0, -2.0, near_tags)
    row_tags = (own_tag[...].astype(jnp.float32), far_tag[...].astype(jnp.float32))
    cacc[...] = jnp.full(cacc.shape, -1.0, jnp.float32)
    col_base = [sum(size for _, _, size in cols[:i]) for i in range(len(cols))]
    for old, new in zip(state_in, state_out):
        new[...] = old[...]
    for r, (which, ref, start, size) in enumerate(rows):
        mine = [c for c in range(len(cols)) if (r, c) in pairs]
        for i in range(0, size, block):
            height = min(block, size - i)
            left = chunks[ref][i : i + height, :]
            tag = []
            for q in range(0, height, LANES):
                line = row_tags[which][(start + i + q) // LANES][None, :]
                tag.append(jnp.broadcast_to(line, (LANES, LANES)).T)
            tag = jnp.concatenate(tag, axis=0)
            best = jnp.full((height, LANES), -1.0, jnp.float32)
            for c in mine:
                col_ref, col_start, col_size = cols[c]
                for j in range(0, col_size, block):
                    width = min(block, col_size - j)
                    right = chunks[col_ref][j : j + width, :]
                    tile = lax.dot_general(
                        left, right, (((1,), (1,)), ((), ())), preferred_element_type=jnp.float32
                    )
                    for g in range(0, width, LANES):
                        line = near_tags[(col_start + j + g) // LANES][None, :]
                        part = jnp.where(tag == line, tile[:, g : g + LANES], -1.0)
                        best = jnp.maximum(best, part)
                        at = col_base[c] + j + g
                        high = jnp.max(part.reshape(height // 8, 8, LANES), axis=0)
                        cacc[:, at : at + LANES] = jnp.maximum(cacc[:, at : at + LANES], high)
            racc[0:height, :] = best
            for q in range(0, height, LANES):
                line = jnp.max(racc[q : q + LANES, :].T, axis=0, keepdims=True)
                at = (start + i + q) // LANES
                state_out[which][at : at + 1, :] = jnp.maximum(state_out[which][at : at + 1, :], line)
    for c, (_, col_start, col_size) in enumerate(cols):
        for j in range(0, col_size, LANES):
            at = col_base[c] + j
            line = jnp.max(cacc[:, at : at + LANES], axis=0, keepdims=True)
            at = (col_start + j) // LANES
            state_out[2][at : at + 1, :] = jnp.maximum(state_out[2][at : at + 1, :], line)


def products(state, tags, own, far, near, want, sizes, block=512):
    starts = [sum(sizes[:i]) for i in range(len(sizes))]
    row_keys = sorted({(w, r) for w, r, _ in want})
    col_keys = sorted({c for _, _, c in want})
    operands, rows, cols = [], [], []
    for which, r in row_keys:
        rows.append((which, len(operands), starts[r], sizes[r]))
        operands.append((own, far)[which][r])
    for c in col_keys:
        cols.append((len(operands), starts[c], sizes[c]))
        operands.append(near[c])
    pairs = frozenset((row_keys.index((w, r)), col_keys.index(c)) for w, r, c in want)
    plan = (tuple(rows), tuple(cols), pairs, block)
    whole = pl.BlockSpec(memory_space=pltpu.VMEM)
    depth = operands[0].shape[1]
    tag_spec = pl.BlockSpec((TAG_ROWS, LANES), lambda i: (sizes[0] // TAG_ROWS, 0))
    data_specs = [pl.BlockSpec(o.shape, lambda i: (0, 0)) for o in operands]
    state_spec = [pl.BlockSpec(s.shape, lambda i: (0, 0)) for s in state]
    macs = sum(sizes[r] * sizes[c] for _, r, c in want)
    kernel = functools.partial(products_kernel, plan, len(operands), 0, 0)
    return pl.pallas_call(
        kernel,
        grid=(1,),
        in_specs=[tag_spec] * 3 + state_spec + data_specs,
        out_specs=state_spec,
        out_shape=[jax.ShapeDtypeStruct(s.shape, s.dtype) for s in state],
        scratch_shapes=[
            pltpu.VMEM((block, LANES), jnp.float32),
            pltpu.VMEM((8, sum(size for _, _, size in cols)), jnp.float32),
        ],
        compiler_params=pltpu.CompilerParams(vmem_limit_bytes=32 << 20),
        cost_estimate=pl.CostEstimate(flops=2 * macs * depth, bytes_accessed=2 * depth * 4096, transcendentals=0),
        name="products",
    )(*tags, *state, *operands)


def per_device(embeddings, cluster_ids, row_counts, *, near_route, far_route):
    rows = embeddings.shape[0]
    sizes = CHUNKS
    back_route = [(b, a) for a, b in near_route]
    ids = cluster_ids.reshape(rows // LANES, LANES)
    own = [normalize(True, 0, sizes[0])(embeddings, row_counts, ids)]
    near = [lax.ppermute(own[0], AXES, near_route)]
    far = [lax.ppermute(own[0], AXES, far_route)]
    start = sizes[0]
    for size in sizes[1:]:
        own.append(normalize(False, start, size)(embeddings))
        near.append(lax.ppermute(own[-1], AXES, near_route))
        far.append(lax.ppermute(own[-1], AXES, far_route))
        start += size
    state = [jnp.full((rows // LANES, LANES), -1.0, jnp.float32)] * 3
    tags = (own[0], far[0], near[0])
    last = len(sizes) - 1
    every = range(len(sizes))
    fold = functools.partial(products, own=own, far=far, near=near, sizes=sizes)
    for c in every:
        want = {(0, r, c) for r in every}
        if c < last:
            want |= {(1, r, c) for r in range(c + 1)}
            want |= {(1, c, k) for k in range(c)}
        else:
            want |= {(1, r, c) for r in range(c)}
        state = fold(state, tags, want=want)
    state = fold(state, tags, want={(1, last, k) for k in every})
    kept, far_best, near_best = [s.reshape(rows) for s in state]
    from_near = lax.ppermute(near_best, AXES, back_route)
    from_far = lax.ppermute(far_best, AXES, far_route)
    return jnp.maximum(kept, jnp.maximum(from_near, from_far))


def solution(mesh):
    near_route, far_route = routes(mesh.shape["grp"], mesh.shape["pair"])
    return jax.shard_map(
        functools.partial(per_device, near_route=near_route, far_route=far_route),
        mesh=mesh,
        in_specs=(P(("grp", "pair"), None), P(("grp", "pair")), P(("grp", "pair"))),
        out_specs=P(("grp", "pair")),
        check_vma=False,
    )
```

```python
import functools

import jax
import jax.numpy as jnp
from jax import lax
from jax.experimental import pallas as pl
from jax.experimental.pallas import tpu as pltpu
from jax.sharding import PartitionSpec as P

LANES = 128
TAG_ROWS = 16
CHUNKS = (768, 512, 256)
AXES = ("grp", "pair")


def routes(grp, pair):
    side = 4
    rest = pair // (side * side)
    near, far = [], []
    for g in range(grp):
        for y in range(side):
            for x in range(side):
                for z in range(rest):

                    def at(v, u):
                        return g * pair + (v * side + u) * rest + z

                    owns_y = (y in (1, 2)) ^ (x in (1, 2)) ^ (g % 2 == 1)
                    here = at(y, x)
                    near.append((here, at(y, x ^ 1) if owns_y else at(y ^ 1, x)))
                    far.append((here, at(3 - y, x) if owns_y else at(y, 3 - x)))
    return near, far


def normalize(rows, first, count, step, row_counts=None, ids=None):
    width = rows.shape[1]
    tagged = ids is not None
    places = [(at, min(step, count - at)) for at in range(0, count, step)]

    def kernel(*refs):
        rows_ref, out_ref, held, arrived = refs[:1] + refs[1 + 2 * tagged : 4 + 2 * tagged]
        copies = [
            pltpu.make_async_copy(rows_ref.at[pl.ds(first + at, size)], held.at[pl.ds(at, size)], arrived.at[i])
            for i, (at, size) in enumerate(places)
        ]
        if tagged:
            valid_ref, ids_ref = refs[1:3]
            held_ids = refs[6]
            ids_copy = pltpu.make_async_copy(ids_ref, held_ids, arrived.at[len(places)])
            ids_copy.start()
        for copy in copies:
            copy.start()
        for copy, (at, size) in zip(copies, places):
            copy.wait()
            wide = held[at : at + size, :].astype(jnp.float32)
            squared = jnp.sum(wide * wide, axis=1, keepdims=True)
            out_ref[at : at + size, :] = (wide * lax.rsqrt(squared + 1e-06)).astype(jnp.bfloat16)
        if tagged:
            ids_copy.wait()
            ids = held_ids[...]
            place = lax.broadcasted_iota(jnp.int32, ids.shape, 0) * LANES
            place = place + lax.broadcasted_iota(jnp.int32, ids.shape, 1)
            tags = jnp.where(place < valid_ref[0], ids, -1).astype(jnp.float32)
            spare = jnp.full((TAG_ROWS - ids.shape[0], LANES), -1.0, jnp.float32)
            out_ref[count:, 0:LANES] = jnp.concatenate([tags, spare], axis=0).astype(jnp.bfloat16)
            out_ref[count:, LANES:] = jnp.zeros((TAG_ROWS, width - LANES), jnp.bfloat16)

    in_hbm = pl.BlockSpec(memory_space=pltpu.HBM)
    total = count + (TAG_ROWS if tagged else 0)
    scratch = [pltpu.VMEM((count, width), jnp.bfloat16), pltpu.SemaphoreType.DMA((len(places) + 1,))]
    if tagged:
        scratch += [pltpu.VMEM(ids.shape, jnp.int32)]
    operands = [pltpu.with_memory_space_constraint(rows, pltpu.HBM)]
    if tagged:
        operands += [row_counts, pltpu.with_memory_space_constraint(ids, pltpu.HBM)]
    return pl.pallas_call(
        kernel,
        in_specs=[in_hbm, pl.BlockSpec(memory_space=pltpu.SMEM), in_hbm] if tagged else [in_hbm],
        out_specs=pl.BlockSpec(memory_space=pltpu.VMEM),
        out_shape=pltpu.VMEM((total, width), jnp.bfloat16),
        scratch_shapes=scratch,
        compiler_params=pltpu.CompilerParams(vmem_limit_bytes=16 << 20),
        cost_estimate=pl.CostEstimate(flops=4 * count * width, bytes_accessed=4 * count * width, transcendentals=count),
        name="normalize",
    )(*operands)


def products_kernel(plan, *refs):
    rows, cols, pairs, touched, tag_at, block, n_chunks = plan
    state_in = dict(zip(touched, refs[: len(touched)]))
    refs = refs[len(touched) :]
    chunks = refs[:n_chunks]
    state_out = dict(zip(touched, refs[n_chunks : n_chunks + len(touched)]))
    cacc = refs[-1]

    def tags_of(which):
        ref, at = tag_at[which]
        return chunks[ref][at : at + TAG_ROWS, 0:LANES].astype(jnp.float32)

    near_tags = tags_of(2)
    near_tags = jnp.where(near_tags < 0.0, -2.0, near_tags)
    row_tags = {which: tags_of(which) for which in {row[0] for row in rows}}
    cacc[...] = jnp.full(cacc.shape, -1.0, jnp.float32)
    for key in touched:
        state_out[key][...] = state_in[key][...]
    for r, (which, ref, start, size) in enumerate(rows):
        mine = [c for c in range(len(cols)) if (r, c) in pairs]
        for i in range(0, size, block):
            height = min(block, size - i)
            left = chunks[ref][i : i + height, :]
            tag = []
            for q in range(0, height, LANES):
                line = row_tags[which][(start + i + q) // LANES][None, :]
                tag.append(jnp.broadcast_to(line, (LANES, LANES)).T)
            tag = jnp.concatenate(tag, axis=0)
            best = jnp.full((height, LANES), -1.0, jnp.float32)
            for c in mine:
                col_ref, col_start, col_size, base = cols[c]
                for j in range(0, col_size, block):
                    width = min(block, col_size - j)
                    right = chunks[col_ref][j : j + width, :]
                    tile = lax.dot_general(
                        left, right, (((1,), (1,)), ((), ())), preferred_element_type=jnp.float32
                    )
                    for g in range(0, width, LANES):
                        line = near_tags[(col_start + j + g) // LANES][None, :]
                        part = jnp.where(tag == line, tile[:, g : g + LANES], -1.0)
                        best = jnp.maximum(best, part)
                        at = base + j + g
                        high = jnp.max(part.reshape(height // 8, 8, LANES), axis=0)
                        cacc[:, at : at + LANES] = jnp.maximum(cacc[:, at : at + LANES], high)
            for q in range(0, height, LANES):
                line = jnp.max(best[q : q + LANES, :].T, axis=0, keepdims=True)
                at = (start + i + q) // LANES
                state_out[which][at : at + 1, :] = jnp.maximum(state_out[which][at : at + 1, :], line)
    for _, col_start, col_size, base in cols:
        for j in range(0, col_size, LANES):
            line = jnp.max(cacc[:, base + j : base + j + LANES], axis=0, keepdims=True)
            at = (col_start + j) // LANES
            state_out[2][at : at + 1, :] = jnp.maximum(state_out[2][at : at + 1, :], line)


def products(state, own, far, near, want, sizes, block=512):
    arrays = (own, far, near)
    starts = [sum(sizes[:i]) for i in range(len(sizes))]
    row_keys = sorted({(w, r) for w, r, _ in want})
    col_keys = sorted({c for _, _, c in want})
    touched = tuple(sorted({w for w, _ in row_keys} | {2}))
    keys = row_keys + [(2, c) for c in col_keys]
    keys += [(w, 0) for w in touched if (w, 0) not in keys]
    rows = tuple((w, keys.index((w, r)), starts[r], sizes[r]) for w, r in row_keys)
    cols = tuple(
        (keys.index((2, c)), starts[c], sizes[c], sum(sizes[k] for k in col_keys[:i])) for i, c in enumerate(col_keys)
    )
    pairs = frozenset((row_keys.index((w, r)), col_keys.index(c)) for w, r, c in want)
    tag_at = {w: (keys.index((w, 0)), sizes[0]) for w in touched}
    plan = (rows, cols, pairs, touched, tag_at, block, len(keys))
    operands = [pltpu.with_memory_space_constraint(arrays[w][c], pltpu.VMEM) for w, c in keys]
    before = [state[w] for w in touched]
    depth = operands[0].shape[1]
    whole = pl.BlockSpec(memory_space=pltpu.VMEM)
    macs = sum(sizes[r] * sizes[c] for _, r, c in want)
    after = pl.pallas_call(
        functools.partial(products_kernel, plan),
        in_specs=[whole] * (len(before) + len(operands)),
        out_specs=[whole] * len(before),
        out_shape=[jax.ShapeDtypeStruct(s.shape, s.dtype) for s in before],
        scratch_shapes=[pltpu.VMEM((8, sum(sizes[c] for c in col_keys)), jnp.float32)],
        compiler_params=pltpu.CompilerParams(vmem_limit_bytes=16 << 20),
        cost_estimate=pl.CostEstimate(flops=2 * macs * depth, bytes_accessed=2 * macs, transcendentals=0),
        name="products",
    )(*before, *operands)
    state = list(state)
    for w, value in zip(touched, after):
        state[w] = value
    return state


def per_device(embeddings, cluster_ids, row_counts, *, near_route, far_route):
    rows = embeddings.shape[0]
    sizes = CHUNKS
    back_route = [(b, a) for a, b in near_route]
    ids = cluster_ids.reshape(rows // LANES, LANES)
    own = [normalize(embeddings, 0, sizes[0], 256, row_counts, ids)]
    far = [lax.ppermute(own[0], AXES, far_route)]
    near = [lax.ppermute(own[0], AXES, near_route)]
    start = sizes[0]
    for size in sizes[1:]:
        embeddings, own[-1] = lax.optimization_barrier((embeddings, own[-1]))
        own.append(normalize(embeddings, start, size, 256))
        far.append(lax.ppermute(own[-1], AXES, far_route))
        near.append(lax.ppermute(own[-1], AXES, near_route))
        start += size
    state = [jnp.full((rows // LANES, LANES), -1.0, jnp.float32)] * 3
    last = len(sizes) - 1
    every = range(len(sizes))
    fold = functools.partial(products, own=own, far=far, near=near, sizes=sizes)
    state = fold(state, want={(0, r, 0) for r in every} | {(1, 0, 0)})
    for c in range(1, last):
        state = fold(state, want={(1, c, k) for k in range(c)})
        state = fold(state, want={(0, r, c) for r in every} | {(1, r, c) for r in range(c + 1)})
    state = fold(state, want={(1, last, k) for k in range(last)})
    state = fold(state, want={(0, r, last) for r in every} | {(1, r, last) for r in every})
    kept, far_best, near_best = [s.reshape(rows) for s in state]
    from_near = lax.ppermute(near_best, AXES, back_route)
    from_far = lax.ppermute(far_best, AXES, far_route)
    return jnp.maximum(kept, jnp.maximum(from_near, from_far))


def solution(mesh):
    near_route, far_route = routes(mesh.shape["grp"], mesh.shape["pair"])
    return jax.shard_map(
        functools.partial(per_device, near_route=near_route, far_route=far_route),
        mesh=mesh,
        in_specs=(P(("grp", "pair"), None), P(("grp", "pair")), P(("grp", "pair"))),
        out_specs=P(("grp", "pair")),
        check_vma=False,
    )
```

```python
import functools

import jax
import jax.numpy as jnp
from jax import lax
from jax.experimental import pallas as pl
from jax.experimental.pallas import tpu as pltpu
from jax.sharding import PartitionSpec as P

LANES = 128
TAG_ROWS = 16
CHUNKS = (768, 512, 256)
AXES = ("grp", "pair")


def routes(grp, pair):
    side = 4
    rest = pair // (side * side)
    near, far = [], []
    for g in range(grp):
        for y in range(side):
            for x in range(side):
                for z in range(rest):

                    def at(v, u):
                        return g * pair + (v * side + u) * rest + z

                    owns_y = (y in (1, 2)) ^ (x in (1, 2)) ^ (g % 2 == 1)
                    here = at(y, x)
                    near.append((here, at(y, x ^ 1) if owns_y else at(y ^ 1, x)))
                    far.append((here, at(3 - y, x) if owns_y else at(y, 3 - x)))
    return near, far


def normalize(rows, first, count, step, row_counts=None, ids=None):
    width = rows.shape[1]
    tagged = ids is not None
    places = [(at, min(step, count - at)) for at in range(0, count, step)]

    def kernel(*refs):
        rows_ref, out_ref, held, arrived = refs[:1] + refs[1 + 2 * tagged : 4 + 2 * tagged]
        copies = [
            pltpu.make_async_copy(rows_ref.at[pl.ds(first + at, size)], held.at[pl.ds(at, size)], arrived.at[i])
            for i, (at, size) in enumerate(places)
        ]
        if tagged:
            valid_ref, ids_ref = refs[1:3]
            held_ids = refs[6]
            ids_copy = pltpu.make_async_copy(ids_ref, held_ids, arrived.at[len(places)])
            ids_copy.start()
        for copy in copies:
            copy.start()
        for copy, (at, size) in zip(copies, places):
            copy.wait()
            wide = held[at : at + size, :].astype(jnp.float32)
            squared = jnp.sum(wide * wide, axis=1, keepdims=True)
            out_ref[at : at + size, :] = (wide * lax.rsqrt(squared + 1e-06)).astype(jnp.bfloat16)
        if tagged:
            ids_copy.wait()
            ids = held_ids[...]
            place = lax.broadcasted_iota(jnp.int32, ids.shape, 0) * LANES
            place = place + lax.broadcasted_iota(jnp.int32, ids.shape, 1)
            tags = jnp.where(place < valid_ref[0], ids, -1).astype(jnp.float32)
            spare = jnp.full((TAG_ROWS - ids.shape[0], LANES), -1.0, jnp.float32)
            out_ref[count:, 0:LANES] = jnp.concatenate([tags, spare], axis=0).astype(jnp.bfloat16)
            out_ref[count:, LANES:] = jnp.zeros((TAG_ROWS, width - LANES), jnp.bfloat16)

    in_hbm = pl.BlockSpec(memory_space=pltpu.HBM)
    total = count + (TAG_ROWS if tagged else 0)
    scratch = [pltpu.VMEM((count, width), jnp.bfloat16), pltpu.SemaphoreType.DMA((len(places) + 1,))]
    if tagged:
        scratch += [pltpu.VMEM(ids.shape, jnp.int32)]
    operands = [pltpu.with_memory_space_constraint(rows, pltpu.HBM)]
    if tagged:
        operands += [row_counts, pltpu.with_memory_space_constraint(ids, pltpu.HBM)]
    return pl.pallas_call(
        kernel,
        in_specs=[in_hbm, pl.BlockSpec(memory_space=pltpu.SMEM), in_hbm] if tagged else [in_hbm],
        out_specs=pl.BlockSpec(memory_space=pltpu.VMEM),
        out_shape=pltpu.VMEM((total, width), jnp.bfloat16),
        scratch_shapes=scratch,
        compiler_params=pltpu.CompilerParams(vmem_limit_bytes=16 << 20),
        cost_estimate=pl.CostEstimate(flops=4 * count * width, bytes_accessed=4 * count * width, transcendentals=count),
        name="normalize",
    )(*operands)


def products_kernel(plan, *refs):
    rows, cols, pairs, touched, tag_at, block, n_chunks = plan
    state_in = dict(zip(touched, refs[: len(touched)]))
    refs = refs[len(touched) :]
    chunks = refs[:n_chunks]
    state_out = dict(zip(touched, refs[n_chunks : n_chunks + len(touched)]))
    cacc = refs[-1]

    def tags_of(which):
        ref, at = tag_at[which]
        return chunks[ref][at : at + TAG_ROWS, 0:LANES].astype(jnp.float32)

    near_tags = tags_of(2)
    near_tags = jnp.where(near_tags < 0.0, -2.0, near_tags)
    row_tags = {which: tags_of(which) for which in {row[0] for row in rows}}
    cacc[...] = jnp.full(cacc.shape, -1.0, jnp.float32)
    for key in touched:
        state_out[key][...] = state_in[key][...]
    for r, (which, ref, start, size) in enumerate(rows):
        mine = [c for c in range(len(cols)) if (r, c) in pairs]
        for i in range(0, size, block):
            height = min(block, size - i)
            left = chunks[ref][i : i + height, :]
            tag = []
            for q in range(0, height, LANES):
                line = row_tags[which][(start + i + q) // LANES][None, :]
                tag.append(jnp.broadcast_to(line, (LANES, LANES)).T)
            tag = jnp.concatenate(tag, axis=0)
            best = jnp.full((height, LANES), -1.0, jnp.float32)
            for c in mine:
                col_ref, col_start, col_size, base = cols[c]
                for j in range(0, col_size, block):
                    width = min(block, col_size - j)
                    right = chunks[col_ref][j : j + width, :]
                    tile = lax.dot_general(
                        left, right, (((1,), (1,)), ((), ())), preferred_element_type=jnp.float32
                    )
                    for g in range(0, width, LANES):
                        line = near_tags[(col_start + j + g) // LANES][None, :]
                        part = jnp.where(tag == line, tile[:, g : g + LANES], -1.0)
                        best = jnp.maximum(best, part)
                        at = base + j + g
                        high = jnp.max(part.reshape(height // 8, 8, LANES), axis=0)
                        cacc[:, at : at + LANES] = jnp.maximum(cacc[:, at : at + LANES], high)
            for q in range(0, height, LANES):
                line = jnp.max(best[q : q + LANES, :].T, axis=0, keepdims=True)
                at = (start + i + q) // LANES
                state_out[which][at : at + 1, :] = jnp.maximum(state_out[which][at : at + 1, :], line)
    for _, col_start, col_size, base in cols:
        for j in range(0, col_size, LANES):
            line = jnp.max(cacc[:, base + j : base + j + LANES], axis=0, keepdims=True)
            at = (col_start + j) // LANES
            state_out[2][at : at + 1, :] = jnp.maximum(state_out[2][at : at + 1, :], line)


def products(state, own, far, near, want, sizes, block=512):
    arrays = (own, far, near)
    starts = [sum(sizes[:i]) for i in range(len(sizes))]
    row_keys = sorted({(w, r) for w, r, _ in want})
    col_keys = sorted({c for _, _, c in want})
    touched = tuple(sorted({w for w, _ in row_keys} | {2}))
    keys = row_keys + [(2, c) for c in col_keys]
    keys += [(w, 0) for w in touched if (w, 0) not in keys]
    rows = tuple((w, keys.index((w, r)), starts[r], sizes[r]) for w, r in row_keys)
    cols = tuple(
        (keys.index((2, c)), starts[c], sizes[c], sum(sizes[k] for k in col_keys[:i])) for i, c in enumerate(col_keys)
    )
    pairs = frozenset((row_keys.index((w, r)), col_keys.index(c)) for w, r, c in want)
    tag_at = {w: (keys.index((w, 0)), sizes[0]) for w in touched}
    plan = (rows, cols, pairs, touched, tag_at, block, len(keys))
    operands = [pltpu.with_memory_space_constraint(arrays[w][c], pltpu.VMEM) for w, c in keys]
    before = [state[w] for w in touched]
    depth = operands[0].shape[1]
    whole = pl.BlockSpec(memory_space=pltpu.VMEM)
    macs = sum(sizes[r] * sizes[c] for _, r, c in want)
    after = pl.pallas_call(
        functools.partial(products_kernel, plan),
        in_specs=[whole] * (len(before) + len(operands)),
        out_specs=[whole] * len(before),
        out_shape=[jax.ShapeDtypeStruct(s.shape, s.dtype) for s in before],
        scratch_shapes=[pltpu.VMEM((8, sum(sizes[c] for c in col_keys)), jnp.float32)],
        compiler_params=pltpu.CompilerParams(vmem_limit_bytes=16 << 20),
        cost_estimate=pl.CostEstimate(flops=2 * macs * depth, bytes_accessed=2 * macs, transcendentals=0),
        name="products",
    )(*before, *operands)
    state = list(state)
    for w, value in zip(touched, after):
        state[w] = value
    return state


def per_device(embeddings, cluster_ids, row_counts, *, near_route, far_route):
    rows = embeddings.shape[0]
    sizes = CHUNKS
    back_route = [(b, a) for a, b in near_route]
    ids = cluster_ids.reshape(rows // LANES, LANES)
    own = [normalize(embeddings, 0, sizes[0], 256, row_counts, ids)]
    far = [lax.ppermute(own[0], AXES, far_route)]
    near = [lax.ppermute(own[0], AXES, near_route)]
    start = sizes[0]
    for size in sizes[1:]:
        embeddings, own[-1] = lax.optimization_barrier((embeddings, own[-1]))
        own.append(normalize(embeddings, start, size, 256))
        far.append(lax.ppermute(own[-1], AXES, far_route))
        near.append(lax.ppermute(own[-1], AXES, near_route))
        start += size
    state = [jnp.full((rows // LANES, LANES), -1.0, jnp.float32)] * 3
    last = len(sizes) - 1
    every = range(len(sizes))
    fold = functools.partial(products, own=own, far=far, near=near, sizes=sizes)
    state = fold(state, want={(0, r, 0) for r in every})
    state = fold(state, want={(1, 0, 0)})
    for c in range(1, len(sizes)):
        state = fold(state, want={(0, r, c) for r in every} | {(1, r, c) for r in range(c)})
        state = fold(state, want={(1, c, k) for k in range(c + 1)})
    kept, far_best, near_best = [s.reshape(rows) for s in state]
    from_near = lax.ppermute(near_best, AXES, back_route)
    from_far = lax.ppermute(far_best, AXES, far_route)
    return jnp.maximum(kept, jnp.maximum(from_near, from_far))


def solution(mesh):
    near_route, far_route = routes(mesh.shape["grp"], mesh.shape["pair"])
    return jax.shard_map(
        functools.partial(per_device, near_route=near_route, far_route=far_route),
        mesh=mesh,
        in_specs=(P(("grp", "pair"), None), P(("grp", "pair")), P(("grp", "pair"))),
        out_specs=P(("grp", "pair")),
        check_vma=False,
    )
```

```python
import functools

import jax
import jax.numpy as jnp
from jax import lax
from jax.experimental import pallas as pl
from jax.experimental.pallas import tpu as pltpu
from jax.sharding import PartitionSpec as P

LANES = 128
TAG_ROWS = 16
CHUNKS = (768, 512, 256)
AXES = ("grp", "pair")


def routes(grp, pair):
    side = 4
    rest = pair // (side * side)
    near, far = [], []
    for g in range(grp):
        for y in range(side):
            for x in range(side):
                for z in range(rest):

                    def at(v, u):
                        return g * pair + (v * side + u) * rest + z

                    owns_y = (y in (1, 2)) ^ (x in (1, 2)) ^ (g % 2 == 1)
                    here = at(y, x)
                    near.append((here, at(y, x ^ 1) if owns_y else at(y ^ 1, x)))
                    far.append((here, at(3 - y, x) if owns_y else at(y, 3 - x)))
    return near, far


def normalize(rows, first, count, step, row_counts=None, ids=None):
    width = rows.shape[1]
    tagged = ids is not None
    places = [(at, min(step, count - at)) for at in range(0, count, step)]

    def kernel(*refs):
        rows_ref, out_ref, held, arrived = refs[:1] + refs[1 + 2 * tagged : 4 + 2 * tagged]
        copies = [
            pltpu.make_async_copy(rows_ref.at[pl.ds(first + at, size)], held.at[pl.ds(at, size)], arrived.at[i])
            for i, (at, size) in enumerate(places)
        ]
        if tagged:
            valid_ref, ids_ref = refs[1:3]
            held_ids = refs[6]
            ids_copy = pltpu.make_async_copy(ids_ref, held_ids, arrived.at[len(places)])
            ids_copy.start()
        for copy in copies:
            copy.start()
        for copy, (at, size) in zip(copies, places):
            copy.wait()
            wide = held[at : at + size, :].astype(jnp.float32)
            squared = jnp.sum(wide * wide, axis=1, keepdims=True)
            out_ref[at : at + size, :] = (wide * lax.rsqrt(squared + 1e-06)).astype(jnp.bfloat16)
        if tagged:
            ids_copy.wait()
            ids = held_ids[...]
            place = lax.broadcasted_iota(jnp.int32, ids.shape, 0) * LANES
            place = place + lax.broadcasted_iota(jnp.int32, ids.shape, 1)
            tags = jnp.where(place < valid_ref[0], ids, -1).astype(jnp.float32)
            spare = jnp.full((TAG_ROWS - ids.shape[0], LANES), -1.0, jnp.float32)
            out_ref[count:, 0:LANES] = jnp.concatenate([tags, spare], axis=0).astype(jnp.bfloat16)
            out_ref[count:, LANES:] = jnp.zeros((TAG_ROWS, width - LANES), jnp.bfloat16)

    in_hbm = pl.BlockSpec(memory_space=pltpu.HBM)
    total = count + (TAG_ROWS if tagged else 0)
    scratch = [pltpu.VMEM((count, width), jnp.bfloat16), pltpu.SemaphoreType.DMA((len(places) + 1,))]
    if tagged:
        scratch += [pltpu.VMEM(ids.shape, jnp.int32)]
    operands = [pltpu.with_memory_space_constraint(rows, pltpu.HBM)]
    if tagged:
        operands += [row_counts, pltpu.with_memory_space_constraint(ids, pltpu.HBM)]
    return pl.pallas_call(
        kernel,
        in_specs=[in_hbm, pl.BlockSpec(memory_space=pltpu.SMEM), in_hbm] if tagged else [in_hbm],
        out_specs=pl.BlockSpec(memory_space=pltpu.VMEM),
        out_shape=pltpu.VMEM((total, width), jnp.bfloat16),
        scratch_shapes=scratch,
        compiler_params=pltpu.CompilerParams(vmem_limit_bytes=16 << 20),
        cost_estimate=pl.CostEstimate(flops=4 * count * width, bytes_accessed=4 * count * width, transcendentals=count),
        name="normalize",
    )(*operands)


def products_kernel(plan, *refs):
    rows, cols, pairs, touched, tag_at, block, n_chunks = plan
    state_in = dict(zip(touched, refs[: len(touched)]))
    refs = refs[len(touched) :]
    chunks = refs[:n_chunks]
    state_out = dict(zip(touched, refs[n_chunks : n_chunks + len(touched)]))
    cacc = refs[-1]

    def tags_of(which):
        ref, at = tag_at[which]
        return chunks[ref][at : at + TAG_ROWS, 0:LANES].astype(jnp.float32)

    near_tags = tags_of(2)
    near_tags = jnp.where(near_tags < 0.0, -2.0, near_tags)
    row_tags = {which: tags_of(which) for which in {row[0] for row in rows}}
    cacc[...] = jnp.full(cacc.shape, -1.0, jnp.float32)
    for key in touched:
        state_out[key][...] = state_in[key][...]
    for r, (which, ref, start, size) in enumerate(rows):
        mine = [c for c in range(len(cols)) if (r, c) in pairs]
        for i in range(0, size, block):
            height = min(block, size - i)
            left = chunks[ref][i : i + height, :]
            tag = []
            for q in range(0, height, LANES):
                line = row_tags[which][(start + i + q) // LANES][None, :]
                tag.append(jnp.broadcast_to(line, (LANES, LANES)).T)
            tag = jnp.concatenate(tag, axis=0)
            best = jnp.full((height, LANES), -1.0, jnp.float32)
            for c in mine:
                col_ref, col_start, col_size, base = cols[c]
                for j in range(0, col_size, block):
                    width = min(block, col_size - j)
                    right = chunks[col_ref][j : j + width, :]
                    tile = lax.dot_general(
                        left, right, (((1,), (1,)), ((), ())), preferred_element_type=jnp.float32
                    )
                    for g in range(0, width, LANES):
                        line = near_tags[(col_start + j + g) // LANES][None, :]
                        part = jnp.where(tag == line, tile[:, g : g + LANES], -1.0)
                        best = jnp.maximum(best, part)
                        at = base + j + g
                        high = jnp.max(part.reshape(height // 8, 8, LANES), axis=0)
                        cacc[:, at : at + LANES] = jnp.maximum(cacc[:, at : at + LANES], high)
            for q in range(0, height, LANES):
                line = jnp.max(best[q : q + LANES, :].T, axis=0, keepdims=True)
                at = (start + i + q) // LANES
                state_out[which][at : at + 1, :] = jnp.maximum(state_out[which][at : at + 1, :], line)
    for _, col_start, col_size, base in cols:
        for j in range(0, col_size, LANES):
            line = jnp.max(cacc[:, base + j : base + j + LANES], axis=0, keepdims=True)
            at = (col_start + j) // LANES
            state_out[2][at : at + 1, :] = jnp.maximum(state_out[2][at : at + 1, :], line)


def products(state, own, far, near, want, sizes, block=512):
    arrays = (own, far, near)
    starts = [sum(sizes[:i]) for i in range(len(sizes))]
    row_keys = sorted({(w, r) for w, r, _ in want})
    col_keys = sorted({c for _, _, c in want})
    touched = tuple(sorted({w for w, _ in row_keys} | {2}))
    keys = row_keys + [(2, c) for c in col_keys]
    keys += [(w, 0) for w in touched if (w, 0) not in keys]
    rows = tuple((w, keys.index((w, r)), starts[r], sizes[r]) for w, r in row_keys)
    cols = tuple(
        (keys.index((2, c)), starts[c], sizes[c], sum(sizes[k] for k in col_keys[:i])) for i, c in enumerate(col_keys)
    )
    pairs = frozenset((row_keys.index((w, r)), col_keys.index(c)) for w, r, c in want)
    tag_at = {w: (keys.index((w, 0)), sizes[0]) for w in touched}
    plan = (rows, cols, pairs, touched, tag_at, block, len(keys))
    operands = [pltpu.with_memory_space_constraint(arrays[w][c], pltpu.VMEM) for w, c in keys]
    before = [state[w] for w in touched]
    depth = operands[0].shape[1]
    whole = pl.BlockSpec(memory_space=pltpu.VMEM)
    macs = sum(sizes[r] * sizes[c] for _, r, c in want)
    after = pl.pallas_call(
        functools.partial(products_kernel, plan),
        in_specs=[whole] * (len(before) + len(operands)),
        out_specs=[whole] * len(before),
        out_shape=[jax.ShapeDtypeStruct(s.shape, s.dtype) for s in before],
        scratch_shapes=[pltpu.VMEM((8, sum(sizes[c] for c in col_keys)), jnp.float32)],
        compiler_params=pltpu.CompilerParams(vmem_limit_bytes=16 << 20),
        cost_estimate=pl.CostEstimate(flops=2 * macs * depth, bytes_accessed=2 * macs, transcendentals=0),
        name="products",
    )(*before, *operands)
    state = list(state)
    for w, value in zip(touched, after):
        state[w] = value
    return state


def per_device(embeddings, cluster_ids, row_counts, *, near_route, far_route):
    rows = embeddings.shape[0]
    sizes = CHUNKS
    back_route = [(b, a) for a, b in near_route]
    ids = cluster_ids.reshape(rows // LANES, LANES)
    own = [normalize(embeddings, 0, sizes[0], 256, row_counts, ids)]
    far = [lax.ppermute(own[0], AXES, far_route)]
    near = [lax.ppermute(own[0], AXES, near_route)]
    start = sizes[0]
    for size in sizes[1:]:
        embeddings, own[-1] = lax.optimization_barrier((embeddings, own[-1]))
        own.append(normalize(embeddings, start, size, 256))
        far.append(lax.ppermute(own[-1], AXES, far_route))
        near.append(lax.ppermute(own[-1], AXES, near_route))
        start += size
    state = [jnp.full((rows // LANES, LANES), -1.0, jnp.float32)] * 3
    last = len(sizes) - 1
    every = range(len(sizes))
    fold = functools.partial(products, own=own, far=far, near=near, sizes=sizes)
    state = fold(state, want={(0, r, 0) for r in every} | {(1, 0, 0)})
    for c in range(1, last):
        state = fold(state, want={(1, c, k) for k in range(c)})
        state = fold(state, want={(0, r, c) for r in every} | {(1, r, c) for r in range(c + 1)})
    state = fold(state, want={(1, last, k) for k in range(last)})
    state = fold(state, want={(0, r, last) for r in every} | {(1, r, last) for r in every})
    kept, far_best, near_best = [s.reshape(rows) for s in state]
    from_far = lax.ppermute(far_best, AXES, far_route)
    from_near = lax.ppermute(near_best, AXES, back_route)
    return jnp.maximum(jnp.maximum(kept, from_near), from_far)


def solution(mesh):
    near_route, far_route = routes(mesh.shape["grp"], mesh.shape["pair"])
    return jax.shard_map(
        functools.partial(per_device, near_route=near_route, far_route=far_route),
        mesh=mesh,
        in_specs=(P(("grp", "pair"), None), P(("grp", "pair")), P(("grp", "pair"))),
        out_specs=P(("grp", "pair")),
        check_vma=False,
    )
```

```python
import functools

import jax
import jax.numpy as jnp
from jax import lax
from jax.experimental import pallas as pl
from jax.experimental.pallas import tpu as pltpu
from jax.sharding import PartitionSpec as P

LANES = 128
TAG_ROWS = 16
CHUNKS = (768, 512, 256)
AXES = ("grp", "pair")


def routes(grp, pair):
    side = 4
    rest = pair // (side * side)
    near, far = [], []
    for g in range(grp):
        for y in range(side):
            for x in range(side):
                for z in range(rest):

                    def at(v, u):
                        return g * pair + (v * side + u) * rest + z

                    owns_y = (y in (1, 2)) ^ (x in (1, 2)) ^ (g % 2 == 1)
                    here = at(y, x)
                    near.append((here, at(y, x ^ 1) if owns_y else at(y ^ 1, x)))
                    far.append((here, at(3 - y, x) if owns_y else at(y, 3 - x)))
    return near, far


def unit_rows(rows):
    wide = rows.astype(jnp.float32)
    squared = jnp.sum(wide * wide, axis=1, keepdims=True)
    return (wide * lax.rsqrt(squared + 1e-06)).astype(jnp.bfloat16)


def head_rows(rows, count, row_counts, ids):
    width = rows.shape[1]

    def kernel(rows_ref, valid_ref, ids_ref, out_ref, held_ids, arrived):
        ids_copy = pltpu.make_async_copy(ids_ref, held_ids, arrived.at[0])
        ids_copy.start()
        copy = pltpu.make_async_copy(rows_ref.at[pl.ds(0, count)], out_ref.at[pl.ds(0, count)], arrived.at[1])
        copy.start()
        ids_copy.wait()
        ids = held_ids[...]
        place = lax.broadcasted_iota(jnp.int32, ids.shape, 0) * LANES
        place = place + lax.broadcasted_iota(jnp.int32, ids.shape, 1)
        tags = jnp.where(place < valid_ref[0], ids, -1).astype(jnp.float32)
        spare = jnp.full((TAG_ROWS - ids.shape[0], LANES), -1.0, jnp.float32)
        out_ref[count:, 0:LANES] = jnp.concatenate([tags, spare], axis=0).astype(jnp.bfloat16)
        out_ref[count:, LANES:] = jnp.zeros((TAG_ROWS, width - LANES), jnp.bfloat16)
        copy.wait()

    in_hbm = pl.BlockSpec(memory_space=pltpu.HBM)
    return pl.pallas_call(
        kernel,
        in_specs=[in_hbm, pl.BlockSpec(memory_space=pltpu.SMEM), in_hbm],
        out_specs=pl.BlockSpec(memory_space=pltpu.VMEM),
        out_shape=pltpu.VMEM((count + TAG_ROWS, width), jnp.bfloat16),
        scratch_shapes=[pltpu.VMEM(ids.shape, jnp.int32), pltpu.SemaphoreType.DMA((2,))],
        cost_estimate=pl.CostEstimate(flops=count, bytes_accessed=4 * count * width, transcendentals=0),
        name="head_rows",
    )(pltpu.with_memory_space_constraint(rows, pltpu.HBM), row_counts, pltpu.with_memory_space_constraint(ids, pltpu.HBM))


def normalize_head(head):
    count, width = head.shape[0] - TAG_ROWS, head.shape[1]

    def kernel(head_ref, out_ref):
        for at in range(0, count, 256):
            out_ref[at : at + 256, :] = unit_rows(head_ref[at : at + 256, :])
        out_ref[count:, :] = head_ref[count:, :]

    whole = pl.BlockSpec(memory_space=pltpu.VMEM)
    return pl.pallas_call(
        kernel,
        in_specs=[whole],
        out_specs=whole,
        out_shape=pltpu.VMEM(head.shape, jnp.bfloat16),
        compiler_params=pltpu.CompilerParams(vmem_limit_bytes=16 << 20),
        cost_estimate=pl.CostEstimate(flops=4 * count * width, bytes_accessed=count * width, transcendentals=count),
        name="normalize_head",
    )(pltpu.with_memory_space_constraint(head, pltpu.VMEM))


def normalize(rows, first, count, step):
    width = rows.shape[1]
    places = [(at, min(step, count - at)) for at in range(0, count, step)]

    def kernel(rows_ref, out_ref, held, arrived):
        copies = [
            pltpu.make_async_copy(rows_ref.at[pl.ds(first + at, size)], held.at[pl.ds(at, size)], arrived.at[i])
            for i, (at, size) in enumerate(places)
        ]
        for copy in copies:
            copy.start()
        for copy, (at, size) in zip(copies, places):
            copy.wait()
            out_ref[at : at + size, :] = unit_rows(held[at : at + size, :])

    return pl.pallas_call(
        kernel,
        in_specs=[pl.BlockSpec(memory_space=pltpu.HBM)],
        out_specs=pl.BlockSpec(memory_space=pltpu.VMEM),
        out_shape=pltpu.VMEM((count, width), jnp.bfloat16),
        scratch_shapes=[pltpu.VMEM((count, width), jnp.bfloat16), pltpu.SemaphoreType.DMA((len(places),))],
        compiler_params=pltpu.CompilerParams(vmem_limit_bytes=16 << 20),
        cost_estimate=pl.CostEstimate(flops=4 * count * width, bytes_accessed=4 * count * width, transcendentals=count),
        name="normalize",
    )(pltpu.with_memory_space_constraint(rows, pltpu.HBM))


def products_kernel(plan, *refs):
    rows, cols, pairs, touched, tag_at, block, n_chunks = plan
    state_in = dict(zip(touched, refs[: len(touched)]))
    refs = refs[len(touched) :]
    chunks = refs[:n_chunks]
    state_out = dict(zip(touched, refs[n_chunks : n_chunks + len(touched)]))
    cacc = refs[-1]

    def tags_of(which):
        ref, at = tag_at[which]
        return chunks[ref][at : at + TAG_ROWS, 0:LANES].astype(jnp.float32)

    row_tags = {which: tags_of(which) for which in {row[0] for row in rows}}
    col_tags = {which: tags_of(which) for which in {col[0] for col in cols}}
    col_tags = {which: jnp.where(tags < 0.0, -2.0, tags) for which, tags in col_tags.items()}
    cacc[...] = jnp.full(cacc.shape, -1.0, jnp.float32)
    for key in touched:
        state_out[key][...] = state_in[key][...]
    for r, (which, ref, start, size) in enumerate(rows):
        mine = [c for c in range(len(cols)) if (r, c) in pairs]
        for i in range(0, size, block):
            height = min(block, size - i)
            left = chunks[ref][i : i + height, :]
            tag = []
            for q in range(0, height, LANES):
                line = row_tags[which][(start + i + q) // LANES][None, :]
                tag.append(jnp.broadcast_to(line, (LANES, LANES)).T)
            tag = jnp.concatenate(tag, axis=0)
            best = jnp.full((height, LANES), -1.0, jnp.float32)
            for c in mine:
                col_which, col_ref, col_start, col_size, base = cols[c]
                for j in range(0, col_size, block):
                    width = min(block, col_size - j)
                    right = chunks[col_ref][j : j + width, :]
                    tile = lax.dot_general(
                        left, right, (((1,), (1,)), ((), ())), preferred_element_type=jnp.float32
                    )
                    for g in range(0, width, LANES):
                        line = col_tags[col_which][(col_start + j + g) // LANES][None, :]
                        part = jnp.where(tag == line, tile[:, g : g + LANES], -1.0)
                        best = jnp.maximum(best, part)
                        at = base + j + g
                        high = jnp.max(part.reshape(height // 8, 8, LANES), axis=0)
                        cacc[:, at : at + LANES] = jnp.maximum(cacc[:, at : at + LANES], high)
            for q in range(0, height, LANES):
                line = jnp.max(best[q : q + LANES, :].T, axis=0, keepdims=True)
                at = (start + i + q) // LANES
                state_out[which][at : at + 1, :] = jnp.maximum(state_out[which][at : at + 1, :], line)
    for which, _, col_start, col_size, base in cols:
        for j in range(0, col_size, LANES):
            line = jnp.max(cacc[:, base + j : base + j + LANES], axis=0, keepdims=True)
            at = (col_start + j) // LANES
            state_out[which][at : at + 1, :] = jnp.maximum(state_out[which][at : at + 1, :], line)


def products(state, want, arrays, sizes, block=512):
    row_keys = sorted({left for left, _ in want})
    col_keys = sorted({right for _, right in want})
    touched = tuple(sorted({w for w, _ in row_keys + col_keys}))
    keys = row_keys + col_keys
    keys += [(w, 0) for w in touched if (w, 0) not in keys]

    def place(key):
        which, chunk = key
        return which, keys.index(key), sum(sizes[which][:chunk]), sizes[which][chunk]

    def width(some):
        return sum(sizes[w][c] for w, c in some)

    rows = tuple(place(key) for key in row_keys)
    cols = tuple(place(key) + (width(col_keys[:i]),) for i, key in enumerate(col_keys))
    pairs = frozenset((row_keys.index(left), col_keys.index(right)) for left, right in want)
    tag_at = {w: (keys.index((w, 0)), sizes[w][0]) for w in touched}
    plan = (rows, cols, pairs, touched, tag_at, block, len(keys))
    operands = [pltpu.with_memory_space_constraint(arrays[w][c], pltpu.VMEM) for w, c in keys]
    before = [state[w] for w in touched]
    depth = operands[0].shape[1]
    whole = pl.BlockSpec(memory_space=pltpu.VMEM)
    macs = sum(width([left]) * width([right]) for left, right in want)
    after = pl.pallas_call(
        functools.partial(products_kernel, plan),
        in_specs=[whole] * (len(before) + len(operands)),
        out_specs=[whole] * len(before),
        out_shape=[jax.ShapeDtypeStruct(s.shape, s.dtype) for s in before],
        scratch_shapes=[pltpu.VMEM((8, width(col_keys)), jnp.float32)],
        compiler_params=pltpu.CompilerParams(vmem_limit_bytes=16 << 20),
        cost_estimate=pl.CostEstimate(flops=2 * macs * depth, bytes_accessed=2 * macs, transcendentals=0),
        name="products",
    )(*before, *operands)
    state = list(state)
    for w, value in zip(touched, after):
        state[w] = value
    return state


def per_device(embeddings, cluster_ids, row_counts, *, near_route, far_route):
    rows = embeddings.shape[0]
    sizes = CHUNKS
    back_route = [(b, a) for a, b in near_route]
    ids = cluster_ids.reshape(rows // LANES, LANES)
    head = head_rows(embeddings, sizes[0], row_counts, ids)
    far = [lax.ppermute(head, AXES, far_route)]
    near = [lax.ppermute(head, AXES, near_route)]
    own = [head]
    start = sizes[0]
    for size in sizes[1:]:
        embeddings, own[-1] = lax.optimization_barrier((embeddings, own[-1]))
        own.append(normalize(embeddings, start, size, 256))
        far.append(lax.ppermute(own[-1], AXES, far_route))
        near.append(lax.ppermute(own[-1], AXES, near_route))
        start += size
    own[0], far[0], near[0] = [normalize_head(h) for h in (own[0], far[0], near[0])]
    state = [jnp.full((rows // LANES, LANES), -1.0, jnp.float32)] * 3
    last = len(sizes) - 1
    every = range(len(sizes))
    fold = functools.partial(products, arrays=(own, far, near), sizes=(sizes,) * 3)
    owns = [(0, r) for r in every]
    fars = [(1, r) for r in every]
    state = fold(state, {(row, (2, 0)) for row in owns + fars[:1]})
    for c in range(1, last):
        state = fold(state, {(fars[c], (2, k)) for k in range(c)})
        state = fold(state, {(row, (2, c)) for row in owns + fars[: c + 1]})
    state = fold(state, {(fars[last], (2, k)) for k in range(last)})
    state = fold(state, {((2, last), col) for col in owns + fars})
    kept, far_best, near_best = [s.reshape(rows) for s in state]
    from_far = lax.ppermute(far_best, AXES, far_route)
    from_near = lax.ppermute(near_best, AXES, back_route)
    return jnp.maximum(jnp.maximum(kept, from_near), from_far)


def solution(mesh):
    near_route, far_route = routes(mesh.shape["grp"], mesh.shape["pair"])
    return jax.shard_map(
        functools.partial(per_device, near_route=near_route, far_route=far_route),
        mesh=mesh,
        in_specs=(P(("grp", "pair"), None), P(("grp", "pair")), P(("grp", "pair"))),
        out_specs=P(("grp", "pair")),
        check_vma=False,
    )
```

```python
import functools

import jax
import jax.numpy as jnp
from jax import lax
from jax.experimental import pallas as pl
from jax.experimental.pallas import tpu as pltpu
from jax.sharding import PartitionSpec as P

LANES = 128
TAG_ROWS = 16
CHUNKS = (768, 512, 256)
AXES = ("grp", "pair")


def routes(grp, pair):
    side = 4
    rest = pair // (side * side)
    near, far = [], []
    for g in range(grp):
        for y in range(side):
            for x in range(side):
                for z in range(rest):

                    def at(v, u):
                        return g * pair + (v * side + u) * rest + z

                    owns_y = (y in (1, 2)) ^ (x in (1, 2)) ^ (g % 2 == 1)
                    here = at(y, x)
                    near.append((here, at(y, x ^ 1) if owns_y else at(y ^ 1, x)))
                    far.append((here, at(3 - y, x) if owns_y else at(y, 3 - x)))
    return near, far


def unit_rows(rows):
    wide = rows.astype(jnp.float32)
    squared = jnp.sum(wide * wide, axis=1, keepdims=True)
    return (wide * lax.rsqrt(squared + 1e-06)).astype(jnp.bfloat16)


def head_rows(rows, count, row_counts, ids):
    width = rows.shape[1]

    def kernel(rows_ref, valid_ref, ids_ref, out_ref, held_ids, arrived):
        ids_copy = pltpu.make_async_copy(ids_ref, held_ids, arrived.at[0])
        ids_copy.start()
        copy = pltpu.make_async_copy(rows_ref.at[pl.ds(0, count)], out_ref.at[pl.ds(0, count)], arrived.at[1])
        copy.start()
        ids_copy.wait()
        ids = held_ids[...]
        place = lax.broadcasted_iota(jnp.int32, ids.shape, 0) * LANES
        place = place + lax.broadcasted_iota(jnp.int32, ids.shape, 1)
        tags = jnp.where(place < valid_ref[0], ids, -1).astype(jnp.float32)
        spare = jnp.full((TAG_ROWS - ids.shape[0], LANES), -1.0, jnp.float32)
        out_ref[count:, 0:LANES] = jnp.concatenate([tags, spare], axis=0).astype(jnp.bfloat16)
        out_ref[count:, LANES:] = jnp.zeros((TAG_ROWS, width - LANES), jnp.bfloat16)
        copy.wait()

    in_hbm = pl.BlockSpec(memory_space=pltpu.HBM)
    return pl.pallas_call(
        kernel,
        in_specs=[in_hbm, pl.BlockSpec(memory_space=pltpu.SMEM), in_hbm],
        out_specs=pl.BlockSpec(memory_space=pltpu.VMEM),
        out_shape=pltpu.VMEM((count + TAG_ROWS, width), jnp.bfloat16),
        scratch_shapes=[pltpu.VMEM(ids.shape, jnp.int32), pltpu.SemaphoreType.DMA((2,))],
        cost_estimate=pl.CostEstimate(flops=count, bytes_accessed=4 * count * width, transcendentals=0),
        name="head_rows",
    )(pltpu.with_memory_space_constraint(rows, pltpu.HBM), row_counts, pltpu.with_memory_space_constraint(ids, pltpu.HBM))


def normalize_head(head):
    count, width = head.shape[0] - TAG_ROWS, head.shape[1]

    def kernel(head_ref, out_ref):
        for at in range(0, count, 256):
            out_ref[at : at + 256, :] = unit_rows(head_ref[at : at + 256, :])
        out_ref[count:, :] = head_ref[count:, :]

    whole = pl.BlockSpec(memory_space=pltpu.VMEM)
    return pl.pallas_call(
        kernel,
        in_specs=[whole],
        out_specs=whole,
        out_shape=pltpu.VMEM(head.shape, jnp.bfloat16),
        compiler_params=pltpu.CompilerParams(vmem_limit_bytes=16 << 20),
        cost_estimate=pl.CostEstimate(flops=4 * count * width, bytes_accessed=count * width, transcendentals=count),
        name="normalize_head",
    )(pltpu.with_memory_space_constraint(head, pltpu.VMEM))


def normalize(rows, first, count, step):
    width = rows.shape[1]
    places = [(at, min(step, count - at)) for at in range(0, count, step)]

    def kernel(rows_ref, out_ref, held, arrived):
        copies = [
            pltpu.make_async_copy(rows_ref.at[pl.ds(first + at, size)], held.at[pl.ds(at, size)], arrived.at[i])
            for i, (at, size) in enumerate(places)
        ]
        for copy in copies:
            copy.start()
        for copy, (at, size) in zip(copies, places):
            copy.wait()
            out_ref[at : at + size, :] = unit_rows(held[at : at + size, :])

    return pl.pallas_call(
        kernel,
        in_specs=[pl.BlockSpec(memory_space=pltpu.HBM)],
        out_specs=pl.BlockSpec(memory_space=pltpu.VMEM),
        out_shape=pltpu.VMEM((count, width), jnp.bfloat16),
        scratch_shapes=[pltpu.VMEM((count, width), jnp.bfloat16), pltpu.SemaphoreType.DMA((len(places),))],
        compiler_params=pltpu.CompilerParams(vmem_limit_bytes=16 << 20),
        cost_estimate=pl.CostEstimate(flops=4 * count * width, bytes_accessed=4 * count * width, transcendentals=count),
        name="normalize",
    )(pltpu.with_memory_space_constraint(rows, pltpu.HBM))


def products_kernel(plan, *refs):
    rows, cols, pairs, touched, tag_at, block, n_chunks = plan
    state_in = dict(zip(touched, refs[: len(touched)]))
    refs = refs[len(touched) :]
    chunks = refs[:n_chunks]
    state_out = dict(zip(touched, refs[n_chunks : n_chunks + len(touched)]))
    cacc = refs[-1]

    def tags_of(which):
        ref, at = tag_at[which]
        return chunks[ref][at : at + TAG_ROWS, 0:LANES].astype(jnp.float32)

    row_tags = {which: tags_of(which) for which in {row[0] for row in rows}}
    col_tags = {which: tags_of(which) for which in {col[0] for col in cols}}
    col_tags = {which: jnp.where(tags < 0.0, -2.0, tags) for which, tags in col_tags.items()}
    cacc[...] = jnp.full(cacc.shape, -1.0, jnp.float32)
    for key in touched:
        state_out[key][...] = state_in[key][...]
    for r, (which, ref, start, size) in enumerate(rows):
        mine = [c for c in range(len(cols)) if (r, c) in pairs]
        for i in range(0, size, block):
            height = min(block, size - i)
            left = chunks[ref][i : i + height, :]
            tag = []
            for q in range(0, height, LANES):
                line = row_tags[which][(start + i + q) // LANES][None, :]
                tag.append(jnp.broadcast_to(line, (LANES, LANES)).T)
            tag = jnp.concatenate(tag, axis=0)
            best = jnp.full((height, LANES), -1.0, jnp.float32)
            for c in mine:
                col_which, col_ref, col_start, col_size, base = cols[c]
                for j in range(0, col_size, block):
                    width = min(block, col_size - j)
                    right = chunks[col_ref][j : j + width, :]
                    tile = lax.dot_general(
                        left, right, (((1,), (1,)), ((), ())), preferred_element_type=jnp.float32
                    )
                    for g in range(0, width, LANES):
                        line = col_tags[col_which][(col_start + j + g) // LANES][None, :]
                        part = jnp.where(tag == line, tile[:, g : g + LANES], -1.0)
                        best = jnp.maximum(best, part)
                        at = base + j + g
                        high = jnp.max(part.reshape(height // 8, 8, LANES), axis=0)
                        cacc[:, at : at + LANES] = jnp.maximum(cacc[:, at : at + LANES], high)
            for q in range(0, height, LANES):
                line = jnp.max(best[q : q + LANES, :].T, axis=0, keepdims=True)
                at = (start + i + q) // LANES
                state_out[which][at : at + 1, :] = jnp.maximum(state_out[which][at : at + 1, :], line)
    for which, _, col_start, col_size, base in cols:
        for j in range(0, col_size, LANES):
            line = jnp.max(cacc[:, base + j : base + j + LANES], axis=0, keepdims=True)
            at = (col_start + j) // LANES
            state_out[which][at : at + 1, :] = jnp.maximum(state_out[which][at : at + 1, :], line)


def products(state, want, arrays, sizes, block=512):
    row_keys = sorted({left for left, _ in want})
    col_keys = sorted({right for _, right in want})
    touched = tuple(sorted({w for w, _ in row_keys + col_keys}))
    keys = row_keys + col_keys
    keys += [(w, 0) for w in touched if (w, 0) not in keys]

    def place(key):
        which, chunk = key
        return which, keys.index(key), sum(sizes[which][:chunk]), sizes[which][chunk]

    def width(some):
        return sum(sizes[w][c] for w, c in some)

    rows = tuple(place(key) for key in row_keys)
    cols = tuple(place(key) + (width(col_keys[:i]),) for i, key in enumerate(col_keys))
    pairs = frozenset((row_keys.index(left), col_keys.index(right)) for left, right in want)
    tag_at = {w: (keys.index((w, 0)), sizes[w][0]) for w in touched}
    plan = (rows, cols, pairs, touched, tag_at, block, len(keys))
    operands = [pltpu.with_memory_space_constraint(arrays[w][c], pltpu.VMEM) for w, c in keys]
    before = [state[w] for w in touched]
    depth = operands[0].shape[1]
    whole = pl.BlockSpec(memory_space=pltpu.VMEM)
    macs = sum(width([left]) * width([right]) for left, right in want)
    after = pl.pallas_call(
        functools.partial(products_kernel, plan),
        in_specs=[whole] * (len(before) + len(operands)),
        out_specs=[whole] * len(before),
        out_shape=[jax.ShapeDtypeStruct(s.shape, s.dtype) for s in before],
        scratch_shapes=[pltpu.VMEM((8, width(col_keys)), jnp.float32)],
        compiler_params=pltpu.CompilerParams(vmem_limit_bytes=16 << 20),
        cost_estimate=pl.CostEstimate(flops=2 * macs * depth, bytes_accessed=2 * macs, transcendentals=0),
        name="products",
    )(*before, *operands)
    state = list(state)
    for w, value in zip(touched, after):
        state[w] = value
    return state


def per_device(embeddings, cluster_ids, row_counts, *, near_route, far_route):
    rows = embeddings.shape[0]
    sizes = CHUNKS
    back_route = [(b, a) for a, b in near_route]
    ids = cluster_ids.reshape(rows // LANES, LANES)
    head = head_rows(embeddings, sizes[0], row_counts, ids)
    far = [lax.ppermute(head, AXES, far_route)]
    near = [lax.ppermute(head, AXES, near_route)]
    own = [head]
    start = sizes[0]
    for size in sizes[1:]:
        embeddings, own[-1] = lax.optimization_barrier((embeddings, own[-1]))
        own.append(normalize(embeddings, start, size, 256))
        far.append(lax.ppermute(own[-1], AXES, far_route))
        near.append(lax.ppermute(own[-1], AXES, near_route))
        start += size
    own[0], far[0], near[0] = [normalize_head(h) for h in (own[0], far[0], near[0])]
    state = [jnp.full((rows // LANES, LANES), -1.0, jnp.float32)] * 3
    last = len(sizes) - 1
    every = range(len(sizes))
    fold = functools.partial(products, arrays=(own, far, near), sizes=(sizes,) * 3)
    owns = [(0, r) for r in every]
    fars = [(1, r) for r in every]
    state = fold(state, {(row, (2, 0)) for row in owns + fars[:1]})
    for c in range(1, last):
        state = fold(state, {(fars[c], (2, k)) for k in range(c)})
        state = fold(state, {(row, (2, c)) for row in owns + fars[: c + 1]})
    state = fold(state, {(fars[last], (2, k)) for k in range(last)})
    state = fold(state, {((2, last), col) for col in owns + fars})
    kept, far_best, near_best = [s.reshape(rows) for s in state]
    from_near = lax.ppermute(near_best, AXES, back_route)
    from_far = lax.ppermute(far_best, AXES, far_route)
    return jnp.maximum(kept, jnp.maximum(from_near, from_far))


def solution(mesh):
    near_route, far_route = routes(mesh.shape["grp"], mesh.shape["pair"])
    return jax.shard_map(
        functools.partial(per_device, near_route=near_route, far_route=far_route),
        mesh=mesh,
        in_specs=(P(("grp", "pair"), None), P(("grp", "pair")), P(("grp", "pair"))),
        out_specs=P(("grp", "pair")),
        check_vma=False,
    )
```
